32 devices in a mesh: dp: 4 (over z), ctx: 8 (over y, x, core).
Axes of the slice: x: 2, y: 2, z: 4, core: 2. Of those that a mesh axis runs over, the one named last changes fastest.
Arguments:
- positions: int32 [3072], P('dp'), parts along dimension 0, may hold values from 0 to 6143, as said below
- queries: bfloat16 [9216, 2048], P(('dp', 'ctx')), parts along dimension 0, may hold values from -12 to 12
- keys_values: bfloat16 [9216, 1024], P(('dp', 'ctx')), parts along dimension 0, may hold values from -12 to 12
- router_weight: bfloat16 [9216], P(('dp', 'ctx')), parts along dimension 0, may hold values from 0.25 to 2
Outputs:
- attended: bfloat16 [9216, 2048], P(('dp', 'ctx')), parts along dimension 0
The draws below stay inside these ranges and needn't reach their ends.
There are 4 independent parts, one for each index of `dp`. The reference program is written for one: setup_inputs(seed, part) draws one part's arguments, and reference() takes and returns one part's arrays. A program takes and returns all parts, laid end to end along the dimension named above; each array names one. Nothing has to cross between parts.
Inputs may be any that keep to these rules, and one draw needn't show every extreme that they name: Distinct and increasing. The shard of positions d * 768 to (d + 1) * 768 - 1 holds at most 288 of them, and one shard holds exactly 288; slots of device d's blocks beyond counts[d] hold data that no output reads.
All inputs are finite; a program needn't handle non-finite values.
Results may differ from the reference program's by a relative error of at most 0.0085.
Values may be sent and summed in bfloat16 or wider, within the bound.
A program may use at most 64 MiB of HBM per device.

```python
import math
import jax
import jax.numpy as jnp
from jax import lax

QUERY_HEADS = 16
KEY_VALUE_HEADS = 4
HEAD_SIZE = 128
TOK_DEV = 768
CAP = 288
SELECTED_TOKENS = 768
N_CTX = 8


def selection_counts(key):
    key_pair = jax.random.split(jax.random.fold_in(key, 5), 2)
    busiest = jax.random.randint(key_pair[0], (), 0, N_CTX)
    shares = jax.random.randint(key_pair[1], (N_CTX,), 1, 4)
    shard_ids = jnp.arange(N_CTX, dtype=jnp.int32)
    others = shard_ids != busiest
    shares = jnp.where(others, shares, 0)
    remaining = SELECTED_TOKENS - CAP
    base_counts = remaining * shares // jnp.sum(shares)
    leftover = remaining - jnp.sum(base_counts)
    order_ids = jnp.cumsum(others.astype(jnp.int32)) - 1
    extra = (others & (order_ids < leftover)).astype(jnp.int32)
    return jnp.where(others, base_counts + extra, CAP).astype(jnp.int32)


def draw_positions(key, part):
    counts = selection_counts(key)
    shard_keys = jax.random.split(jax.random.fold_in(key, 7), N_CTX)

    def shard_mask(shard_key, shard_count):
        shuffled = jax.random.permutation(shard_key, TOK_DEV)
        chosen = (jnp.arange(TOK_DEV, dtype=jnp.int32) < shard_count).astype(jnp.int32)
        return jnp.zeros((TOK_DEV,), jnp.int32).at[shuffled].set(chosen)
    full_mask = jax.vmap(shard_mask)(shard_keys, counts).reshape(-1)
    ordering = jnp.argsort(1 - full_mask, stable=True)
    return ordering[:SELECTED_TOKENS].astype(jnp.int32)


def attention_inputs(key):
    base_key = jax.random.fold_in(key, 11)
    key_block_list = jax.random.split(base_key, 3)
    overall_row_count = N_CTX * CAP
    group_count = QUERY_HEADS // KEY_VALUE_HEADS
    unprojected_queries = jnp.clip(jax.random.normal(key_block_list[0], (overall_row_count, KEY_VALUE_HEADS, group_count, HEAD_SIZE), jnp.float32), -6.0, 6.0)
    unprojected_keys = jnp.clip(jax.random.normal(key_block_list[1], (overall_row_count, KEY_VALUE_HEADS, HEAD_SIZE), jnp.float32), -6.0, 6.0)
    unprojected_values = jnp.clip(jax.random.normal(key_block_list[2], (overall_row_count, KEY_VALUE_HEADS, HEAD_SIZE), jnp.float32), -6.0, 6.0)
    queries = unprojected_queries.reshape(overall_row_count, QUERY_HEADS * HEAD_SIZE).astype(jnp.bfloat16)
    stacked_blocks = jnp.concatenate([unprojected_keys.reshape(overall_row_count, KEY_VALUE_HEADS * HEAD_SIZE), unprojected_values.reshape(overall_row_count, KEY_VALUE_HEADS * HEAD_SIZE)], axis=1)
    return (queries, stacked_blocks.astype(jnp.bfloat16))


def draw_queries(key, part):
    return attention_inputs(key)[0]


def draw_keys_values(key, part):
    return attention_inputs(key)[1]


def shard_levels(stream_key, extent, shards, low, high):
    def one(axis_at, shards_of):
        draws = jax.random.uniform(jax.random.fold_in(jax.random.fold_in(stream_key, 6), axis_at), (shards_of,), jnp.float32, low / len(shards), high / len(shards))
        return jnp.repeat(jnp.exp(draws), extent[axis_at] // shards_of).reshape((-1,) + (1,) * (len(extent) - axis_at - 1))

    gain = one(*shards[0])
    for cut in shards[1:]:
        gain = gain * one(*cut)
    return gain


def setup_inputs(seed: int = 0, part: int = 0) -> dict:
    seeds = jax.random.split(jax.random.key(seed), 5)
    part_splits = jax.random.split(jax.random.fold_in(seeds[4], part), 5)
    positions = draw_positions(jax.random.fold_in(jax.random.fold_in(seeds[4], part), 71), part)
    queries = draw_queries(jax.random.fold_in(jax.random.fold_in(seeds[4], part), 71), part)
    keys_values = draw_keys_values(jax.random.fold_in(jax.random.fold_in(seeds[4], part), 71), part)
    router_weight = jnp.clip(jnp.exp(math.log(2.0) - 2.0794415 * jax.random.uniform(part_splits[3], (N_CTX * CAP,), jnp.float32) ** shard_levels(part_splits[3], (N_CTX * CAP,), ((0, 8),), -0.2, 0.2)), 0.25, 2.0).astype(jnp.bfloat16)
    return {"positions": positions, "queries": queries, "keys_values": keys_values, "router_weight": router_weight}


def reference(positions, queries, keys_values, router_weight):
    bounds = jnp.arange(N_CTX + 1, dtype=jnp.int32) * TOK_DEV
    offsets = lax.optimization_barrier(jnp.sum((positions[None, :] < bounds[:, None]).astype(jnp.int32), axis=1)).astype(jnp.int32)
    starts = offsets[:-1]
    counts = offsets[1:] - starts
    global_idx = jnp.arange(SELECTED_TOKENS, dtype=jnp.int32)
    owners = lax.optimization_barrier(jnp.sum((offsets[None, 1:] <= global_idx[:, None]).astype(jnp.int32), axis=1)).astype(jnp.int32)
    source_rows = (owners * CAP + global_idx - jnp.take(starts, owners)).astype(jnp.int32)
    sel_queries = jnp.take(queries, source_rows, axis=0)
    selected_key_value = jnp.take(keys_values, source_rows, axis=0)
    sel_gate = jnp.take(router_weight, source_rows, axis=0)
    group_count = QUERY_HEADS // KEY_VALUE_HEADS
    every_key_row = selected_key_value[:, :KEY_VALUE_HEADS * HEAD_SIZE].reshape(SELECTED_TOKENS, KEY_VALUE_HEADS, HEAD_SIZE).astype(jnp.float32)
    every_value_row = selected_key_value[:, KEY_VALUE_HEADS * HEAD_SIZE:].reshape(SELECTED_TOKENS, KEY_VALUE_HEADS, HEAD_SIZE).astype(jnp.float32)
    query_block_start = math.gcd(SELECTED_TOKENS, 512)
    num_blocks = SELECTED_TOKENS // query_block_start
    score_scale = 1.0 / math.sqrt(HEAD_SIZE)

    def one_block(block_id):
        first = block_id * query_block_start
        query_row_count = lax.dynamic_slice_in_dim(sel_queries, first, query_block_start, 0)
        query_row_count = query_row_count.reshape(query_block_start, KEY_VALUE_HEADS, group_count, HEAD_SIZE).astype(jnp.float32)
        scores = jnp.einsum('qkgd,ckd->kgqc', query_row_count, every_key_row) * score_scale
        query_index = first + jnp.arange(query_block_start, dtype=jnp.int32)
        visible = global_idx[None, :] <= query_index[:, None]
        masked = jnp.where(visible, scores, -1e+30)
        row_max = lax.optimization_barrier(jnp.max(masked, axis=-1))
        weights = jnp.where(visible, jnp.exp(masked - row_max[..., None]), 0.0)
        totals = lax.optimization_barrier(jnp.sum(weights, axis=-1))
        rounded = lax.optimization_barrier(weights.astype(jnp.bfloat16)).astype(jnp.float32)
        weighted = jnp.einsum('kgqc,ckd->qkgd', rounded, every_value_row)
        weighted = weighted / jnp.transpose(totals, (2, 0, 1))[..., None]
        return weighted.reshape(query_block_start, QUERY_HEADS * HEAD_SIZE)
    attended_sel = lax.map(one_block, jnp.arange(num_blocks, dtype=jnp.int32)).reshape(SELECTED_TOKENS, QUERY_HEADS * HEAD_SIZE)
    scaled = sel_gate.astype(jnp.float32)[:, None] * attended_sel
    slot_rows = jnp.arange(N_CTX * CAP, dtype=jnp.int32)
    shard_ids = slot_rows // CAP
    slot_ids = slot_rows % CAP
    live_slot = slot_ids < jnp.take(counts, shard_ids)
    target_rows = jnp.clip(jnp.take(starts, shard_ids) + slot_ids, 0, SELECTED_TOKENS - 1).astype(jnp.int32)
    picked = jnp.take(scaled, target_rows, axis=0)
    return jnp.where(live_slot[:, None], picked, 0.0).astype(jnp.bfloat16)
```

```python
import functools
import math

import jax
import jax.numpy as jnp
from jax import lax
from jax.experimental import pallas as pl
from jax.experimental.pallas import tpu as pltpu
from jax.sharding import PartitionSpec as P

HEAD_SIZE = 128
TOK_DEV = 768
PIECES = 2
MASKED = -1e30


def kernel(
    n,
    positions_ref,
    queries_ref,
    kv_ref,
    gate_ref,
    out_ref,
    queries,
    gathered,
    placing,
    packed,
    accum,
    maxima,
    bias,
    local_sem,
    spread_send,
    spread_recv,
    share_send,
    share_recv,
    pass_send,
    pass_recv,
):
    me = lax.axis_index("ctx")
    chip, core = me // 2, lax.rem(me, 2)
    chips = n // 2
    partner = me + 1 - 2 * core
    slots = kv_ref.shape[0]
    strips = kv_ref.shape[1] // HEAD_SIZE
    kv_heads = strips // 2
    group = queries_ref.shape[1] // HEAD_SIZE // kv_heads
    total = positions_ref.shape[1]
    rows = total // (n // strips)
    piece = rows // PIECES

    def strip_of(device):
        return lax.rem(device, strips)

    def place_of(device, p):
        start = pl.multiple_of((device // strips) * rows + p * piece, 16)
        return packed.at[strip_of(device), pl.ds(start, piece), :]

    def columns(strip):
        return pl.ds(pl.multiple_of(strip * HEAD_SIZE, HEAD_SIZE), HEAD_SIZE)

    load_queries = pltpu.make_async_copy(queries_ref, queries, local_sem.at[0])
    load_queries.start()
    my_slots = pl.ds(pl.multiple_of(me * slots, 16), slots)
    keep = pltpu.make_async_copy(
        kv_ref.at[:, columns(strip_of(me))], gathered.at[my_slots, :], local_sem.at[1]
    )
    keep.start()

    barrier = pltpu.get_barrier_semaphore()
    for o in range(1, n):
        pl.semaphore_signal(
            barrier,
            inc=1,
            device_id={"ctx": lax.rem(me + o, n)},
            device_id_type=pl.DeviceIdType.MESH,
        )
    pl.semaphore_wait(barrier, n - 1)

    spread = []
    for o in range(1, n):
        target = lax.rem(me + o, n)
        copy = pltpu.make_async_remote_copy(
            src_ref=kv_ref.at[:, columns(strip_of(target))],
            dst_ref=gathered.at[my_slots, :],
            send_sem=spread_send.at[o],
            recv_sem=spread_recv.at[o],
            device_id={"ctx": target},
            device_id_type=pl.DeviceIdType.MESH,
        )
        copy.start()
        spread.append(copy)

    positions = positions_ref[...]

    def below(bound):
        hit = jnp.where(positions < bound, 1.0, 0.0)
        return jnp.sum(hit, axis=1, keepdims=True).astype(jnp.int32)

    base = (me // strips) * rows
    shard = lax.broadcasted_iota(jnp.int32, (n, 1), 0)
    starts, ends = below(shard * TOK_DEV), below((shard + 1) * TOK_DEV)
    slot = lax.broadcasted_iota(jnp.int32, (n, slots), 1)
    shift = jnp.where(slot < ends - starts, starts - base, -(2**24))
    distance = lax.broadcasted_iota(jnp.int32, (rows, slots), 0) - lax.broadcasted_iota(
        jnp.int32, (rows, slots), 1
    )
    for s in range(n):
        placing[s] = jnp.where(distance == shift[s : s + 1, :], 1.0, 0.0).astype(jnp.bfloat16)

    my_start, my_end = below(me * TOK_DEV), below((me + 1) * TOK_DEV)
    across = lax.broadcasted_iota(jnp.int32, (slots, slots), 1)
    down = lax.broadcasted_iota(jnp.int32, (slots, slots), 0)
    gate = jnp.sum(
        jnp.where(across == down, gate_ref[...].astype(jnp.float32), 0.0), axis=1, keepdims=True
    )
    live = down[:, :1] < my_end - my_start

    keep.wait()
    for copy in spread:
        copy.wait_recv()

    sends = list(spread)
    share, forward = {}, {}

    def send(p, source, target, send_sem, recv_sem):
        ref = place_of(source, p)
        copy = pltpu.make_async_remote_copy(
            src_ref=ref,
            dst_ref=ref,
            send_sem=send_sem,
            recv_sem=recv_sem,
            device_id={"ctx": target},
            device_id_type=pl.DeviceIdType.MESH,
        )
        copy.start()
        return copy

    for p in range(PIECES):
        strip = jnp.zeros((piece, HEAD_SIZE), jnp.float32)
        for s in range(n):
            strip += jnp.dot(
                placing[s, p * piece : (p + 1) * piece, :],
                gathered[s * slots : (s + 1) * slots, :],
                preferred_element_type=jnp.float32,
            )
        mine = pl.ds(pl.multiple_of(base + p * piece, 16), piece)
        packed[strip_of(me), mine, :] = strip.astype(jnp.bfloat16)
        for o in range(1, chips):
            target = lax.rem(chip + o, chips) * 2 + core
            share[p, o] = send(p, me, target, share_send.at[p, o], share_recv.at[p, o])
        share[p, 0] = send(p, me, partner, share_send.at[p, 0], share_recv.at[p, 0])

    factor = math.log2(math.e) / math.sqrt(HEAD_SIZE)
    ones = jnp.ones((piece, HEAD_SIZE), jnp.bfloat16)
    load_queries.wait()
    key_at = lax.broadcasted_iota(jnp.int32, (slots, piece), 1) - lax.broadcasted_iota(
        jnp.int32, (slots, piece), 0
    )

    def attend(start, first, last):
        bias[...] = jnp.where(key_at <= my_start - start, 0.0, MASKED)
        span = slice(start, start + piece)

        def one_head(h, carry):
            keys = packed[h, span, :]
            values = jnp.concatenate([packed[kv_heads + h, span, :], ones], axis=1)
            for g in range(group):
                head = h * group + g
                scores = lax.dot_general(
                    queries[:, columns(head)],
                    keys,
                    (((1,), (1,)), ((), ())),
                    preferred_element_type=jnp.float32,
                )
                scores = scores * factor + bias[...]
                top = jnp.max(scores, axis=1, keepdims=True)
                if not first:
                    before = maxima[head][:, :1]
                    top = jnp.maximum(top, before)
                weights = jnp.exp2(scores - top).astype(jnp.bfloat16)
                mixed = jnp.dot(weights, values, preferred_element_type=jnp.float32)
                if not first:
                    mixed += accum[head] * jnp.exp2(before - top)
                if last:
                    result = mixed[:, :HEAD_SIZE] / mixed[:, HEAD_SIZE:] * gate
                    out_ref[:, columns(head)] = jnp.where(live, result, 0.0).astype(out_ref.dtype)
                else:
                    accum[head] = mixed
                    maxima[head] = jnp.broadcast_to(top, (slots, HEAD_SIZE))
            return carry

        lax.fori_loop(0, kv_heads, one_head, 0)

    for p in range(PIECES):
        for o in range(1, chips):
            share[p, o].wait_recv()
            source = lax.rem(chip + chips - o, chips) * 2 + core
            forward[p, o] = send(p, source, partner, pass_send.at[p, o], pass_recv.at[p, o])
        share[p, 0].wait_recv()
        for o in range(1, chips):
            forward[p, o].wait_recv()
        parts = n // strips
        for r in range(parts):
            attend(
                r * rows + p * piece,
                first=p == 0 and r == 0,
                last=p == PIECES - 1 and r == parts - 1,
            )

    for copy in sends + list(share.values()) + list(forward.values()):
        copy.wait_send()


def per_device(n, positions, queries, keys_values, router_weight):
    slots, width = queries.shape
    total = positions.shape[0]
    strips = keys_values.shape[1] // HEAD_SIZE
    rows = total // (n // strips)
    piece = rows // PIECES
    heads = width // HEAD_SIZE
    chips = n // 2
    vmem = pl.BlockSpec(memory_space=pltpu.VMEM)
    anywhere = pl.BlockSpec(memory_space=pl.ANY)
    dma = pltpu.SemaphoreType.DMA
    return pl.pallas_call(
        functools.partial(kernel, n),
        out_shape=jax.ShapeDtypeStruct((slots, width), jnp.bfloat16),
        in_specs=[vmem, anywhere, anywhere, vmem],
        out_specs=vmem,
        scratch_shapes=[
            pltpu.VMEM((slots, width), jnp.bfloat16),
            pltpu.VMEM((n * slots, HEAD_SIZE), jnp.bfloat16),
            pltpu.VMEM((n, rows, slots), jnp.bfloat16),
            pltpu.VMEM((strips, total, HEAD_SIZE), jnp.bfloat16),
            pltpu.VMEM((heads, slots, 2 * HEAD_SIZE), jnp.float32),
            pltpu.VMEM((heads, slots, HEAD_SIZE), jnp.float32),
            pltpu.VMEM((slots, piece), jnp.float32),
            dma((2,)),
            dma((n,)),
            dma((n,)),
            dma((PIECES, chips)),
            dma((PIECES, chips)),
            dma((PIECES, chips)),
            dma((PIECES, chips)),
        ],
        compiler_params=pltpu.CompilerParams(
            collective_id=0, has_side_effects=True, vmem_limit_bytes=56 * 2**20
        ),
        cost_estimate=pl.CostEstimate(
            flops=4 * slots * total * width,
            bytes_accessed=4 * slots * width + 2 * total * strips * HEAD_SIZE,
            transcendentals=slots * total * heads,
        ),
    )(positions.reshape(1, total), queries, keys_values, router_weight.reshape(1, slots))


def solution(mesh):
    in_specs = (P("dp"), P(("dp", "ctx"), None), P(("dp", "ctx"), None), P(("dp", "ctx")))
    out_specs = P(("dp", "ctx"), None)
    return jax.shard_map(
        functools.partial(per_device, mesh.shape["ctx"]),
        mesh=mesh,
        in_specs=in_specs,
        out_specs=out_specs,
        check_vma=False,
    )
```

```python
import functools
import math

import jax
import jax.numpy as jnp
from jax import lax
from jax.experimental import pallas as pl
from jax.experimental.pallas import tpu as pltpu
from jax.sharding import PartitionSpec as P

HEAD_SIZE = 128
TOK_DEV = 768
PIECES = 2
MASKED = -1e30


def kernel(
    n,
    positions_ref,
    queries_ref,
    kv_ref,
    gate_ref,
    out_ref,
    queries,
    gathered,
    placing,
    packed,
    accum,
    maxima,
    bias,
    local_sem,
    spread_send,
    spread_recv,
    share_send,
    share_recv,
    pass_send,
    pass_recv,
):
    me = lax.axis_index("ctx")
    chip, core = me // 2, lax.rem(me, 2)
    chips = n // 2
    partner = me + 1 - 2 * core
    slots = kv_ref.shape[0]
    strips = kv_ref.shape[1] // HEAD_SIZE
    kv_heads = strips // 2
    heads = queries_ref.shape[1] // HEAD_SIZE
    group = heads // kv_heads
    total = positions_ref.shape[0]
    rows = total // (n // strips)
    piece = rows // PIECES

    def strip_of(device):
        return lax.rem(device, strips)

    def place_of(device, p):
        start = pl.multiple_of((device // strips) * rows + p * piece, 16)
        return packed.at[strip_of(device), pl.ds(start, piece), :]

    def columns(strip):
        return pl.ds(pl.multiple_of(strip * HEAD_SIZE, HEAD_SIZE), HEAD_SIZE)

    load_queries = [
        pltpu.make_async_copy(queries_ref.at[:, columns(i)], queries.at[i], local_sem.at[i])
        for i in range(heads)
    ]
    my_slots = pl.ds(pl.multiple_of(me * slots, 16), slots)
    keep = pltpu.make_async_copy(
        kv_ref.at[:, columns(strip_of(me))], gathered.at[my_slots, :], local_sem.at[heads]
    )
    keep.start()

    barrier = pltpu.get_barrier_semaphore()
    for o in range(1, n):
        pl.semaphore_signal(
            barrier,
            inc=1,
            device_id={"ctx": lax.rem(me + o, n)},
            device_id_type=pl.DeviceIdType.MESH,
        )
    pl.semaphore_wait(barrier, n - 1)

    spread = []
    for o in range(1, n):
        target = lax.rem(me + o, n)
        copy = pltpu.make_async_remote_copy(
            src_ref=kv_ref.at[:, columns(strip_of(target))],
            dst_ref=gathered.at[my_slots, :],
            send_sem=spread_send.at[o],
            recv_sem=spread_recv.at[o],
            device_id={"ctx": target},
            device_id_type=pl.DeviceIdType.MESH,
        )
        copy.start()
        spread.append(copy)
    for copy in load_queries:
        copy.start()

    positions = positions_ref[...].reshape(1, total)

    def below(bound):
        hit = jnp.where(positions < bound, 1.0, 0.0)
        return jnp.sum(hit, axis=1, keepdims=True).astype(jnp.int32)

    base = (me // strips) * rows
    shard = lax.broadcasted_iota(jnp.int32, (n, 1), 0)
    starts, ends = below(shard * TOK_DEV), below((shard + 1) * TOK_DEV)
    slot = lax.broadcasted_iota(jnp.int32, (n, slots), 1)
    shift = jnp.where(slot < ends - starts, starts - base, -(2**24))
    distance = lax.broadcasted_iota(jnp.int32, (rows, slots), 0) - lax.broadcasted_iota(
        jnp.int32, (rows, slots), 1
    )
    for s in range(n):
        placing[s] = jnp.where(distance == shift[s : s + 1, :], 1.0, 0.0).astype(jnp.bfloat16)

    my_start, my_end = below(me * TOK_DEV), below((me + 1) * TOK_DEV)
    across = lax.broadcasted_iota(jnp.int32, (slots, slots), 1)
    down = lax.broadcasted_iota(jnp.int32, (slots, slots), 0)
    gate = jnp.sum(
        jnp.where(across == down, gate_ref[...].astype(jnp.float32).reshape(1, slots), 0.0), axis=1, keepdims=True
    )
    live = down[:, :1] < my_end - my_start

    keep.wait()
    for copy in spread:
        copy.wait_recv()

    sends = list(spread)
    share, forward = {}, {}

    def send(p, source, target, send_sem, recv_sem):
        ref = place_of(source, p)
        copy = pltpu.make_async_remote_copy(
            src_ref=ref,
            dst_ref=ref,
            send_sem=send_sem,
            recv_sem=recv_sem,
            device_id={"ctx": target},
            device_id_type=pl.DeviceIdType.MESH,
        )
        copy.start()
        return copy

    for p in range(PIECES):
        strip = jnp.zeros((piece, HEAD_SIZE), jnp.float32)
        for s in range(n):
            strip += jnp.dot(
                placing[s, p * piece : (p + 1) * piece, :],
                gathered[s * slots : (s + 1) * slots, :],
                preferred_element_type=jnp.float32,
            )
        mine = pl.ds(pl.multiple_of(base + p * piece, 16), piece)
        packed[strip_of(me), mine, :] = strip.astype(jnp.bfloat16)
        for o in range(1, chips):
            target = lax.rem(chip + o, chips) * 2 + core
            share[p, o] = send(p, me, target, share_send.at[p, o], share_recv.at[p, o])
        share[p, 0] = send(p, me, partner, share_send.at[p, 0], share_recv.at[p, 0])

    factor = math.log2(math.e) / math.sqrt(HEAD_SIZE)
    ones = jnp.ones((piece, HEAD_SIZE), jnp.bfloat16)
    for copy in load_queries:
        copy.wait()
    key_at = lax.broadcasted_iota(jnp.int32, (slots, piece), 1) - lax.broadcasted_iota(
        jnp.int32, (slots, piece), 0
    )

    def attend(start, first, last):
        bias[...] = jnp.where(key_at <= my_start - start, 0.0, MASKED)
        span = slice(start, start + piece)

        def one_head(h, carry):
            keys = packed[h, span, :]
            values = jnp.concatenate([packed[kv_heads + h, span, :], ones], axis=1)
            mine = pl.ds(h * group, group)
            scores = lax.dot_general(
                queries[mine].reshape(group * slots, HEAD_SIZE),
                keys,
                (((1,), (1,)), ((), ())),
                preferred_element_type=jnp.float32,
            )
            scores = scores.reshape(group, slots, piece) * factor + bias[...]
            top = jnp.max(scores, axis=2, keepdims=True)
            if not first:
                before = maxima[mine][:, :, :1]
                top = jnp.maximum(top, before)
            weights = jnp.exp2(scores - top).astype(jnp.bfloat16)
            mixed = jnp.dot(
                weights.reshape(group * slots, piece), values, preferred_element_type=jnp.float32
            ).reshape(group, slots, 2 * HEAD_SIZE)
            if not first:
                mixed += accum[mine] * jnp.exp2(before - top)
            if last:
                result = mixed[:, :, :HEAD_SIZE] / mixed[:, :, HEAD_SIZE:] * gate
                result = jnp.where(live, result, 0.0).astype(out_ref.dtype)
                for g in range(group):
                    out_ref[:, columns(h * group + g)] = result[g]
            else:
                accum[mine] = mixed
                maxima[mine] = jnp.broadcast_to(top, (group, slots, HEAD_SIZE))
            return carry

        lax.fori_loop(0, kv_heads, one_head, 0)

    for p in range(PIECES):
        for o in range(1, chips):
            share[p, o].wait_recv()
            source = lax.rem(chip + chips - o, chips) * 2 + core
            forward[p, o] = send(p, source, partner, pass_send.at[p, o], pass_recv.at[p, o])
        share[p, 0].wait_recv()
        for o in range(1, chips):
            forward[p, o].wait_recv()
        parts = n // strips
        for r in range(parts):
            attend(
                r * rows + p * piece,
                first=p == 0 and r == 0,
                last=p == PIECES - 1 and r == parts - 1,
            )

    for copy in sends + list(share.values()) + list(forward.values()):
        copy.wait_send()


def write_out(attended_ref, out_ref, sem):
    copy = pltpu.make_async_copy(attended_ref, out_ref, sem)
    copy.start()
    copy.wait()


def per_device(n, positions, queries, keys_values, router_weight):
    slots, width = queries.shape
    total = positions.shape[0]
    strips = keys_values.shape[1] // HEAD_SIZE
    rows = total // (n // strips)
    piece = rows // PIECES
    heads = width // HEAD_SIZE
    chips = n // 2
    vmem = pl.BlockSpec(memory_space=pltpu.VMEM)
    anywhere = pl.BlockSpec(memory_space=pl.ANY)
    dma = pltpu.SemaphoreType.DMA
    attended = pl.pallas_call(
        functools.partial(kernel, n),
        out_shape=jax.ShapeDtypeStruct((slots, width), jnp.bfloat16),
        in_specs=[vmem, anywhere, anywhere, vmem],
        out_specs=vmem,
        scratch_shapes=[
            pltpu.VMEM((heads, slots, HEAD_SIZE), jnp.bfloat16),
            pltpu.VMEM((n * slots, HEAD_SIZE), jnp.bfloat16),
            pltpu.VMEM((n, rows, slots), jnp.bfloat16),
            pltpu.VMEM((strips, total, HEAD_SIZE), jnp.bfloat16),
            pltpu.VMEM((heads, slots, 2 * HEAD_SIZE), jnp.float32),
            pltpu.VMEM((heads, slots, HEAD_SIZE), jnp.float32),
            pltpu.VMEM((slots, piece), jnp.float32),
            dma((heads + 1,)),
            dma((n,)),
            dma((n,)),
            dma((PIECES, chips)),
            dma((PIECES, chips)),
            dma((PIECES, chips)),
            dma((PIECES, chips)),
        ],
        compiler_params=pltpu.CompilerParams(
            collective_id=0, has_side_effects=True, vmem_limit_bytes=56 * 2**20
        ),
        cost_estimate=pl.CostEstimate(
            flops=4 * slots * total * width,
            bytes_accessed=4 * slots * width + 2 * total * strips * HEAD_SIZE,
            transcendentals=slots * total * heads,
        ),
    )(positions, queries, keys_values, router_weight)

    return pl.pallas_call(
        write_out,
        out_shape=jax.ShapeDtypeStruct((slots, width), jnp.bfloat16),
        in_specs=[anywhere],
        out_specs=anywhere,
        scratch_shapes=[dma],
    )(attended)


def solution(mesh):
    in_specs = (P("dp"), P(("dp", "ctx"), None), P(("dp", "ctx"), None), P(("dp", "ctx")))
    out_specs = P(("dp", "ctx"), None)
    return jax.shard_map(
        functools.partial(per_device, mesh.shape["ctx"]),
        mesh=mesh,
        in_specs=in_specs,
        out_specs=out_specs,
        check_vma=False,
    )
```

```python
import functools
import math

import jax
import jax.numpy as jnp
from jax import lax
from jax.experimental import pallas as pl
from jax.experimental.pallas import tpu as pltpu
from jax.sharding import PartitionSpec as P

HEAD_SIZE = 128
TOK_DEV = 768
PIECES = 2
MASKED = -1e30


def kernel(
    n,
    positions_ref,
    queries_ref,
    kv_ref,
    gate_ref,
    out_ref,
    queries,
    gathered,
    placing,
    packed,
    accum,
    maxima,
    bias,
    local_sem,
    spread_send,
    spread_recv,
    share_send,
    share_recv,
    pass_send,
    pass_recv,
):
    me = lax.axis_index("ctx")
    chip, core = me // 2, lax.rem(me, 2)
    chips = n // 2
    partner = me + 1 - 2 * core
    slots = kv_ref.shape[0]
    strips = kv_ref.shape[1] // HEAD_SIZE
    kv_heads = strips // 2
    heads = queries_ref.shape[1] // HEAD_SIZE
    group = heads // kv_heads
    total = positions_ref.shape[0]
    rows = total // (n // strips)
    piece = rows // PIECES

    def strip_of(device):
        return lax.rem(device, strips)

    def place_of(device, p):
        start = pl.multiple_of((device // strips) * rows + p * piece, 16)
        return packed.at[strip_of(device), pl.ds(start, piece), :]

    def columns(strip):
        return pl.ds(pl.multiple_of(strip * HEAD_SIZE, HEAD_SIZE), HEAD_SIZE)

    load_queries = [
        pltpu.make_async_copy(queries_ref.at[:, columns(i)], queries.at[i], local_sem.at[i])
        for i in range(heads)
    ]
    my_slots = pl.ds(pl.multiple_of(me * slots, 16), slots)
    keep = pltpu.make_async_copy(
        kv_ref.at[:, columns(strip_of(me))], gathered.at[my_slots, :], local_sem.at[heads]
    )
    keep.start()

    barrier = pltpu.get_barrier_semaphore()
    for o in range(1, n):
        pl.semaphore_signal(
            barrier,
            inc=1,
            device_id={"ctx": lax.rem(me + o, n)},
            device_id_type=pl.DeviceIdType.MESH,
        )
    pl.semaphore_wait(barrier, n - 1)

    spread = []
    for o in range(1, n):
        target = lax.rem(me + o, n)
        copy = pltpu.make_async_remote_copy(
            src_ref=kv_ref.at[:, columns(strip_of(target))],
            dst_ref=gathered.at[my_slots, :],
            send_sem=spread_send.at[o],
            recv_sem=spread_recv.at[o],
            device_id={"ctx": target},
            device_id_type=pl.DeviceIdType.MESH,
        )
        copy.start()
        spread.append(copy)
    for copy in load_queries:
        copy.start()

    positions = positions_ref[...].reshape(1, total)

    def below(bound):
        hit = jnp.where(positions < bound, 1.0, 0.0)
        return jnp.sum(hit, axis=1, keepdims=True).astype(jnp.int32)

    base = (me // strips) * rows
    shard = lax.broadcasted_iota(jnp.int32, (n, 1), 0)
    starts, ends = below(shard * TOK_DEV), below((shard + 1) * TOK_DEV)
    slot = lax.broadcasted_iota(jnp.int32, (n, slots), 1)
    shift = jnp.where(slot < ends - starts, starts - base, -(2**24))
    distance = lax.broadcasted_iota(jnp.int32, (rows, slots), 0) - lax.broadcasted_iota(
        jnp.int32, (rows, slots), 1
    )
    for s in range(n):
        placing[s] = jnp.where(distance == shift[s : s + 1, :], 1.0, 0.0).astype(jnp.bfloat16)

    my_start, my_end = below(me * TOK_DEV), below((me + 1) * TOK_DEV)
    across = lax.broadcasted_iota(jnp.int32, (slots, slots), 1)
    down = lax.broadcasted_iota(jnp.int32, (slots, slots), 0)
    gate = jnp.sum(
        jnp.where(across == down, gate_ref[...].astype(jnp.float32).reshape(1, slots), 0.0), axis=1, keepdims=True
    )
    live = down[:, :1] < my_end - my_start

    keep.wait()
    for copy in spread:
        copy.wait_recv()

    sends = list(spread)
    share, forward = {}, {}

    def send(p, source, target, send_sem, recv_sem):
        ref = place_of(source, p)
        copy = pltpu.make_async_remote_copy(
            src_ref=ref,
            dst_ref=ref,
            send_sem=send_sem,
            recv_sem=recv_sem,
            device_id={"ctx": target},
            device_id_type=pl.DeviceIdType.MESH,
        )
        copy.start()
        return copy

    for p in range(PIECES):
        strip = jnp.zeros((piece, HEAD_SIZE), jnp.float32)
        for s in range(n):
            strip += jnp.dot(
                placing[s, p * piece : (p + 1) * piece, :],
                gathered[s * slots : (s + 1) * slots, :],
                preferred_element_type=jnp.float32,
            )
        mine = pl.ds(pl.multiple_of(base + p * piece, 16), piece)
        packed[strip_of(me), mine, :] = strip.astype(jnp.bfloat16)
        for o in range(1, chips):
            target = lax.rem(chip + o, chips) * 2 + core
            share[p, o] = send(p, me, target, share_send.at[p, o], share_recv.at[p, o])
        share[p, 0] = send(p, me, partner, share_send.at[p, 0], share_recv.at[p, 0])

    factor = math.log2(math.e) / math.sqrt(HEAD_SIZE)
    ones = jnp.ones((piece, HEAD_SIZE), jnp.bfloat16)
    for copy in load_queries:
        copy.wait()
    key_at = lax.broadcasted_iota(jnp.int32, (slots, piece), 1) - lax.broadcasted_iota(
        jnp.int32, (slots, piece), 0
    )

    def attend(start, first, last):
        bias[...] = jnp.where(key_at <= my_start - start, 0.0, MASKED)
        span = slice(start, start + piece)

        def one_head(h, carry):
            keys = packed[h, span, :]
            values = jnp.concatenate([packed[kv_heads + h, span, :], ones], axis=1)
            mine = pl.ds(h * group, group)
            scores = lax.dot_general(
                queries[mine].reshape(group * slots, HEAD_SIZE),
                keys,
                (((1,), (1,)), ((), ())),
                preferred_element_type=jnp.float32,
            )
            scores = scores.reshape(group, slots, piece) * factor + bias[...]
            top = jnp.max(scores, axis=2, keepdims=True)
            if not first:
                before = maxima[mine][:, :, :1]
                top = jnp.maximum(top, before)
            weights = jnp.exp2(scores - top).astype(jnp.bfloat16)
            mixed = jnp.dot(
                weights.reshape(group * slots, piece), values, preferred_element_type=jnp.float32
            ).reshape(group, slots, 2 * HEAD_SIZE)
            if not first:
                mixed += accum[mine] * jnp.exp2(before - top)
            if last:
                result = mixed[:, :, :HEAD_SIZE] / mixed[:, :, HEAD_SIZE:] * gate
                result = jnp.where(live, result, 0.0).astype(out_ref.dtype)
                for g in range(group):
                    out_ref[:, columns(h * group + g)] = result[g]
            else:
                accum[mine] = mixed
                maxima[mine] = jnp.broadcast_to(top, (group, slots, HEAD_SIZE))
            return carry

        lax.fori_loop(0, kv_heads, one_head, 0)

    for p in range(PIECES):
        for o in range(1, chips):
            share[p, o].wait_recv()
            source = lax.rem(chip + chips - o, chips) * 2 + core
            forward[p, o] = send(p, source, partner, pass_send.at[p, o], pass_recv.at[p, o])
        share[p, 0].wait_recv()
        for o in range(1, chips):
            forward[p, o].wait_recv()
        parts = n // strips
        for r in range(parts):
            attend(
                r * rows + p * piece,
                first=p == 0 and r == 0,
                last=p == PIECES - 1 and r == parts - 1,
            )

    for copy in sends + list(share.values()) + list(forward.values()):
        copy.wait_send()


def write_out(parts, attended_ref, out_ref, held, load_sem, store_sem):
    size = attended_ref.shape[0] // parts
    loads, stores = [], []
    for i in range(parts):
        span = pl.ds(i * size, size)
        loads.append(
            pltpu.make_async_copy(attended_ref.at[span], held.at[span], load_sem.at[i])
        )
        stores.append(pltpu.make_async_copy(held.at[span], out_ref.at[span], store_sem.at[i]))
    for copy in loads:
        copy.start()
    for load, store in zip(loads, stores):
        load.wait()
        store.start()
    for copy in stores:
        copy.wait()


def per_device(n, positions, queries, keys_values, router_weight):
    slots, width = queries.shape
    total = positions.shape[0]
    strips = keys_values.shape[1] // HEAD_SIZE
    rows = total // (n // strips)
    piece = rows // PIECES
    heads = width // HEAD_SIZE
    chips = n // 2
    vmem = pl.BlockSpec(memory_space=pltpu.VMEM)
    anywhere = pl.BlockSpec(memory_space=pl.ANY)
    dma = pltpu.SemaphoreType.DMA
    attended = pl.pallas_call(
        functools.partial(kernel, n),
        out_shape=jax.ShapeDtypeStruct((slots, width), jnp.bfloat16),
        in_specs=[vmem, anywhere, anywhere, vmem],
        out_specs=vmem,
        scratch_shapes=[
            pltpu.VMEM((heads, slots, HEAD_SIZE), jnp.bfloat16),
            pltpu.VMEM((n * slots, HEAD_SIZE), jnp.bfloat16),
            pltpu.VMEM((n, rows, slots), jnp.bfloat16),
            pltpu.VMEM((strips, total, HEAD_SIZE), jnp.bfloat16),
            pltpu.VMEM((heads, slots, 2 * HEAD_SIZE), jnp.float32),
            pltpu.VMEM((heads, slots, HEAD_SIZE), jnp.float32),
            pltpu.VMEM((slots, piece), jnp.float32),
            dma((heads + 1,)),
            dma((n,)),
            dma((n,)),
            dma((PIECES, chips)),
            dma((PIECES, chips)),
            dma((PIECES, chips)),
            dma((PIECES, chips)),
        ],
        compiler_params=pltpu.CompilerParams(
            collective_id=0, has_side_effects=True, vmem_limit_bytes=56 * 2**20
        ),
        cost_estimate=pl.CostEstimate(
            flops=4 * slots * total * width,
            bytes_accessed=4 * slots * width + 2 * total * strips * HEAD_SIZE,
            transcendentals=slots * total * heads,
        ),
    )(positions, queries, keys_values, router_weight)

    parts = math.gcd(slots // 16, 6)
    return pl.pallas_call(
        functools.partial(write_out, parts),
        out_shape=jax.ShapeDtypeStruct((slots, width), jnp.bfloat16),
        in_specs=[anywhere],
        out_specs=anywhere,
        scratch_shapes=[
            pltpu.VMEM((slots, width), jnp.bfloat16),
            dma((parts,)),
            dma((parts,)),
        ],
    )(attended)


def solution(mesh):
    in_specs = (P("dp"), P(("dp", "ctx"), None), P(("dp", "ctx"), None), P(("dp", "ctx")))
    out_specs = P(("dp", "ctx"), None)
    return jax.shard_map(
        functools.partial(per_device, mesh.shape["ctx"]),
        mesh=mesh,
        in_specs=in_specs,
        out_specs=out_specs,
        check_vma=False,
    )
```
